32 devices in a mesh: grp: 2 (over y), row: 8 (over z, x), col: 2 (over core).
Axes of the slice: x: 2, y: 2, z: 4, core: 2. Of those that a mesh axis runs over, the one named last changes fastest.
Arguments:
- queries: bfloat16 [1024, 8192], P(('grp', 'row'), 'col'), parts along dimension 0, may hold values from -256 to 256
- key_cache: bfloat16 [512, 512], P(('grp', 'row', 'col')), parts along dimension 0, may hold values from -6 to 6
- value_cache: bfloat16 [512, 512], P(('grp', 'row', 'col')), parts along dimension 0, may hold values from -6 to 6
- tile_active: int32 [8, 2], P('grp'), parts along dimension 0, may hold values from 0 to 1, as said below
- query_step: int32 [1024], P(('grp', 'row')), parts along dimension 0, may hold values from 0 to 63
- key_step: int32 [512], P(('grp', 'row', 'col')), parts along dimension 0, may hold values from 0 to 63, never falling along the last dimension, each value on 1 to 16 neighbouring positions
Outputs:
- attended: bfloat16 [1024, 8192], P(('grp', 'row'), 'col'), parts along dimension 0
The draws below stay inside these ranges and needn't reach their ends.
There are 2 independent parts, one for each index of `grp`. The reference program is written for one: setup_inputs(seed, part) draws one part's arguments, and reference() takes and returns one part's arrays. A program takes and returns all parts, laid end to end along the dimension named above; each array names one. Nothing has to cross between parts.
Inputs may be any that keep to these rules, and one draw needn't show every extreme that they name: `tile_active`: every entry of column 0 is 1. `key_step`: never falls along the cached rows and starts at 0.
All inputs are finite; a program needn't handle non-finite values.
Results may differ from the reference program's by a relative error of at most 0.015.
Values may be sent and summed in bfloat16 or wider, within the bound.
A program may use at most 64 MiB of HBM per device.

```python
import math
import jax
import jax.numpy as jnp
import numpy as np
from jax import lax

H = 64
KVH = 4
DH = 128
TILE = 128
STEPS = 64
QROWS = 512
KEYS = 256


def cache_values(key):
    source = jax.random.fold_in(key, 11)
    result = jnp.clip(jax.random.normal(source, (KEYS, KVH * DH), jnp.float32), -6.0, 6.0)
    return result


def draw_key_cache(key, part):
    return cache_values(key).astype(jnp.bfloat16)


def draw_queries(key, part):
    noise = jnp.clip(jax.random.normal(jax.random.fold_in(key, 23), (QROWS, H * DH), jnp.float32), -6.0, 6.0)
    return noise.astype(jnp.bfloat16)


def draw_tile_active(key, part):
    tiles_query = QROWS // TILE
    tiles_key = KEYS // TILE
    limits = jax.random.randint(jax.random.fold_in(key, 31), (tiles_query, 1), tiles_key // 4, tiles_key + 1)
    holes = jax.random.randint(jax.random.fold_in(key, 37), (tiles_query, tiles_key), 0, 8)
    positions = jnp.arange(tiles_key, dtype=jnp.int32)[None, :]
    active = (positions < limits) & (holes != 0) | (positions == 0)
    return active.astype(jnp.int32)


def with_ends(entries, own_key, least, top_value):
    index_at = [jax.random.randint(jax.random.fold_in(own_key, axis), (), 0, length) for axis, length in enumerate(entries.shape)]
    longest = entries.shape.index(max(entries.shape))
    next_to = index_at[:longest] + [(index_at[longest] + 1) % entries.shape[longest]] + index_at[longest + 1:]
    return entries.at[tuple(index_at)].set(least).at[tuple(next_to)].set(top_value)


def level_of(own_key, dims, shards, smallest, largest):
    def one(dim, parts):
        steps = jax.random.uniform(jax.random.fold_in(jax.random.fold_in(own_key, 6), dim), (parts,), jnp.float32, smallest / len(shards), largest / len(shards))
        return jnp.repeat(jnp.exp(steps), dims[dim] // parts).reshape((-1,) + (1,) * (len(dims) - dim - 1))

    loudness = one(*shards[0])
    for cut in shards[1:]:
        loudness = loudness * one(*cut)
    return loudness


def profile(count, total, limit, slope):
    portions = [(1 << 20) // math.isqrt(standing ** slope) + 1 for standing in range(2, count + 1)]
    spare, holding = total - limit - (count - 1), [1] * (count - 1)
    while spare > 0:
        movable = [i for i in range(count - 1) if holding[i] < limit]
        whole, left = sum([portions[i] for i in movable]), spare
        for i in movable:
            addition = min(limit - holding[i], max(1, left * portions[i] // whole), spare)
            holding[i] = holding[i] + addition
            spare = spare - addition
    return np.array([limit] + holding)


def ragged(rng, count, total, most, skew):
    if count == 2:
        one = jax.random.randint(rng, (), max(1, total - most), min(most, total - 1) + 1)
        return jnp.stack([one, total - one])
    sizes = jnp.asarray(profile(count, total, most, skew), jnp.int32)
    twos = (count - 1) // 2
    donor, sink = sizes[1:1 + 2 * twos:2], sizes[2:2 + 2 * twos:2]
    room = jnp.minimum(donor - 1, most - sink)
    passed = jax.random.randint(jax.random.fold_in(rng, 1), (twos,), 0, 1 << 20) % (room + 1)
    sizes = sizes.at[1:1 + 2 * twos:2].set(donor - passed).at[2:2 + 2 * twos:2].set(sink + passed)
    return sizes[jax.random.permutation(jax.random.fold_in(rng, 2), count)]


def centred(stream_key, dims, width, limit, split=(), held_as=jnp.bfloat16):
    loudness = level_of(stream_key, dims, split, -0.22, 0.18) if split else 1.0
    entries = jax.random.normal(stream_key, dims, jnp.float32) * width * loudness
    return jnp.minimum(jnp.maximum(entries, -limit), limit).astype(held_as)


def setup_inputs(seed: int = 0, part: int = 0) -> dict:
    streams_of = jax.random.split(jax.random.key(seed), 7)
    part_keys = jax.random.split(jax.random.fold_in(streams_of[6], part), 7)
    queries = draw_queries(jax.random.fold_in(jax.random.fold_in(streams_of[6], part), 71), part)
    key_cache = draw_key_cache(jax.random.fold_in(jax.random.fold_in(streams_of[6], part), 71), part)
    value_cache = centred(part_keys[2], (KEYS, KVH * DH), 1.0, 6.0, ((0, 16),))
    tile_active = draw_tile_active(jax.random.fold_in(jax.random.fold_in(streams_of[6], part), 71), part)
    query_step = with_ends(jax.random.randint(part_keys[4], (QROWS,), 0, STEPS), jax.random.fold_in(part_keys[4], 1), 0, STEPS - 1).astype(jnp.int32)
    key_step = jnp.searchsorted(jnp.cumsum(ragged(part_keys[5], STEPS, KEYS, KEYS // 16, 2)), jnp.arange(KEYS), side="right").astype(jnp.int32)
    return {"queries": queries, "key_cache": key_cache, "value_cache": value_cache, "tile_active": tile_active, "query_step": query_step, "key_step": key_step}


def reference(queries, key_cache, value_cache, tile_active, query_step, key_step):
    groups = H // KVH
    scaling = 1.0 / math.sqrt(DH)
    tile_count = QROWS // TILE
    key_tiles = jnp.arange(KEYS, dtype=jnp.int32) // TILE
    keys_wide = key_cache.astype(jnp.float32).reshape(KEYS, KVH, DH)
    values_wide = value_cache.astype(jnp.float32).reshape(KEYS, KVH, DH)

    def one_tile(inputs):
        query_block, steps_block, tile_row = inputs
        heads = query_block.astype(jnp.float32).reshape(TILE, KVH, groups, DH)
        scores = jnp.einsum('qhgd,khd->hgqk', heads, keys_wide) * scaling
        allowed = (tile_row[key_tiles] == 1)[None, :] & (key_step[None, :] <= steps_block[:, None])
        scores = jnp.where(allowed[None, None], scores, -jnp.inf)
        highest = lax.optimization_barrier(jnp.max(scores, axis=-1, keepdims=True))
        weights = jnp.exp(scores - highest)
        totals = lax.optimization_barrier(jnp.sum(weights, axis=-1))
        rounded = lax.optimization_barrier(weights.astype(jnp.bfloat16)).astype(jnp.float32)
        numerator = jnp.einsum('hgqk,khd->hgqd', rounded, values_wide)
        result = numerator / totals[..., None]
        return result.transpose(2, 0, 1, 3).reshape(TILE, H * DH).astype(jnp.bfloat16)
    blocks = lax.map(one_tile, (queries.reshape(tile_count, TILE, H * DH), query_step.reshape(tile_count, TILE), tile_active))
    return blocks.reshape(QROWS, H * DH)
```

```python
import functools
import math

import jax
import jax.numpy as jnp
from jax import lax
from jax.experimental import pallas as pl
from jax.experimental.pallas import tpu as pltpu
from jax.sharding import PartitionSpec as P

H = 64
KVH = 4
DH = 128
TILE = 128
STEPS = 64
LOW = -1e30
MESH = pl.DeviceIdType.MESH


def repeat(count, body):
    if count <= 32:
        for index in range(count):
            body(index)
    else:
        lax.fori_loop(0, count, lambda index, nothing: (body(index), nothing)[1], 0)


def attend(q, kv_ref, bias_ref, head, heads, peers, scale):
    depth = kv_ref.shape[1]
    rows = q.shape[0]
    copies = rows // bias_ref.shape[0]
    span = min(peers, max(1, 512 // depth))

    def piece(first):
        keys = kv_ref[pl.ds(first, span), :, head * DH : (head + 1) * DH]
        values = kv_ref[pl.ds(first, span), :, (heads + head) * DH : (heads + head + 1) * DH]
        keys = keys.reshape(span * depth, DH)
        values = values.reshape(span * depth, DH)
        values = jnp.concatenate([values, jnp.ones_like(values)], axis=1)
        scores = lax.dot_general(q, keys, (((1,), (1,)), ((), ())), preferred_element_type=jnp.float32)
        return scores * scale, values

    if span == peers:
        scores, values = piece(0)
        bias = bias_ref[...]
        scores = scores + jnp.concatenate([bias] * copies, axis=0)
        top = jnp.max(scores, axis=1, keepdims=True)
        weights = jnp.exp2(scores - top).astype(jnp.bfloat16)
        both = jnp.dot(weights, values, preferred_element_type=jnp.float32)
    else:
        width = span * depth

        def step(index, carry):
            top, both = carry
            scores, values = piece(index * span)
            bias = bias_ref[:, pl.ds(pl.multiple_of(index * width, width), width)]
            scores = scores + jnp.concatenate([bias] * copies, axis=0)
            newest = jnp.maximum(top, jnp.max(scores, axis=1, keepdims=True))
            weights = jnp.where(scores > 0.5 * LOW, jnp.exp2(scores - newest), 0.0).astype(jnp.bfloat16)
            both = both * jnp.exp2(top - newest) + jnp.dot(weights, values, preferred_element_type=jnp.float32)
            return newest, both

        top = jnp.full((rows, 1), LOW, jnp.float32)
        top, both = lax.fori_loop(0, peers // span, step, (top, jnp.zeros((rows, 2 * DH), jnp.float32)))
    return both[:, :DH] / both[:, DH:]


def kernel(
    row_count, columns, q_hbm, k_ref, v_ref, tile_ref, qstep_ref, kstep_ref, out_ref,
    q_ref, send_ref, kv_ref, bias_ref, q_sem, send_sem, recv_sem,
):
    peers = row_count * columns
    heads = KVH // columns
    half = heads * DH
    groups = H // KVH
    depth = k_ref.shape[0]
    keys = peers * depth
    query_count = q_ref.shape[0]
    row = lax.axis_index("row")
    col = lax.axis_index("col")
    me = row * columns + col

    q_copy = pltpu.make_async_copy(q_hbm, q_ref, q_sem)
    q_copy.start()

    def place(distance):
        peer = lax.rem(me + distance + 1, peers)
        return peer, peer // columns, lax.rem(peer, columns)

    barrier = pltpu.get_barrier_semaphore()

    def greet(distance):
        peer, peer_row, peer_col = place(distance)
        pl.semaphore_signal(barrier, inc=1, device_id={"row": peer_row, "col": peer_col}, device_id_type=MESH)

    repeat(peers - 1, greet)

    steps = kstep_ref[...].astype(jnp.float32)
    eye = lax.broadcasted_iota(jnp.int32, (depth, depth), 0) == lax.broadcasted_iota(jnp.int32, (depth, depth), 1)
    column = jnp.sum(jnp.where(eye, jnp.broadcast_to(steps, (depth, depth)), 0.0), axis=1, keepdims=True)
    marks = jnp.broadcast_to(column, (depth, DH)).astype(jnp.bfloat16)
    for other in range(columns):
        send_ref[other, :, :half] = k_ref[:, other * half : (other + 1) * half]
        send_ref[other, :, half : 2 * half] = v_ref[:, other * half : (other + 1) * half]
        send_ref[other, :, 2 * half :] = marks
    kv_ref[me] = send_ref[col]

    pl.semaphore_wait(barrier, peers - 1)

    def copy_to(peer, peer_row, peer_col):
        return pltpu.make_async_remote_copy(
            src_ref=send_ref.at[peer_col],
            dst_ref=kv_ref.at[me],
            send_sem=send_sem.at[peer],
            recv_sem=recv_sem.at[me],
            device_id={"row": peer_row, "col": peer_col},
            device_id_type=MESH,
        )

    repeat(peers - 1, lambda distance: copy_to(*place(distance)).start())

    def receive(distance):
        peer, peer_row, peer_col = place(distance)
        pltpu.make_async_remote_copy(
            src_ref=send_ref.at[0],
            dst_ref=kv_ref.at[peer],
            send_sem=send_sem.at[peer],
            recv_sem=recv_sem.at[peer],
            device_id={"row": peer_row, "col": peer_col},
            device_id_type=MESH,
        ).wait_recv()

    q_copy.wait()
    repeat(peers - 1, receive)

    marks = kv_ref[:, :, 2 * half :].reshape(keys, DH).astype(jnp.float32)
    lane = lax.broadcasted_iota(jnp.int32, (keys, DH), 1).astype(jnp.float32)
    late = jnp.where(marks > lane, LOW, 0.0).astype(jnp.bfloat16)
    picked = lax.broadcasted_iota(jnp.int32, (DH, query_count), 0) == qstep_ref[...]
    picked = jnp.where(picked, 1.0, 0.0).astype(jnp.bfloat16)
    bias = lax.dot_general(picked, late, (((0,), (1,)), ((), ())), preferred_element_type=jnp.float32)
    first_row = row * query_count
    key_tiles = tile_ref.shape[1]
    block = min(TILE, query_count)
    for part in range(query_count // block):
        tile = (first_row + part * block) // TILE
        for key_tile in range(key_tiles):
            closed = jnp.where(tile_ref[tile, key_tile] == 1, 0.0, LOW)
            span = slice(key_tile * TILE, (key_tile + 1) * TILE)
            bias_ref[part * block : (part + 1) * block, span] = (
                bias[part * block : (part + 1) * block, span] + closed
            )

    scale = math.log2(math.e) / math.sqrt(DH)
    together = max(1, min(groups, 256 // query_count))
    for head in range(heads):
        for start in range(0, groups, together):
            base = (head * groups + start) * DH
            q = jnp.concatenate(
                [q_ref[:, base + g * DH : base + (g + 1) * DH] for g in range(together)], axis=0
            )
            result = attend(q, kv_ref, bias_ref, head, heads, peers, scale).astype(jnp.bfloat16)
            for g in range(together):
                out_ref[:, base + g * DH : base + (g + 1) * DH] = result[
                    g * query_count : (g + 1) * query_count
                ]

    repeat(peers - 1, lambda distance: copy_to(*place(distance)).wait_send())


def solution(mesh):
    row_count, columns = mesh.shape["row"], mesh.shape["col"]
    peers = row_count * columns

    def per_device(queries, key_cache, value_cache, tile_active, query_step, key_step):
        depth = key_cache.shape[0]
        width = 2 * (KVH // columns) * DH + DH
        vmem = pl.BlockSpec(memory_space=pltpu.VMEM)
        return pl.pallas_call(
            functools.partial(kernel, row_count, columns),
            out_shape=jax.ShapeDtypeStruct(queries.shape, jnp.bfloat16),
            in_specs=[
                pl.BlockSpec(memory_space=pl.ANY),
                vmem,
                vmem,
                pl.BlockSpec(memory_space=pltpu.SMEM),
                vmem,
                vmem,
            ],
            out_specs=vmem,
            scratch_shapes=[
                pltpu.VMEM(queries.shape, jnp.bfloat16),
                pltpu.VMEM((columns, depth, width), jnp.bfloat16),
                pltpu.VMEM((peers, depth, width), jnp.bfloat16),
                pltpu.VMEM((queries.shape[0], peers * depth), jnp.float32),
                pltpu.SemaphoreType.DMA,
                pltpu.SemaphoreType.DMA((peers,)),
                pltpu.SemaphoreType.DMA((peers,)),
            ],
            compiler_params=pltpu.CompilerParams(
                collective_id=0, has_side_effects=True, vmem_limit_bytes=48 * 1024 * 1024
            ),
        )(queries, key_cache, value_cache, tile_active, query_step[None, :], key_step[None, :])

    in_specs = (
        P(("grp", "row"), "col"),
        P(("grp", "row", "col"), None),
        P(("grp", "row", "col"), None),
        P("grp", None),
        P(("grp", "row")),
        P(("grp", "row", "col")),
    )
    return jax.shard_map(
        per_device, mesh=mesh, in_specs=in_specs, out_specs=P(("grp", "row"), "col"), check_vma=False
    )
```

```python
import functools
import math

import jax
import jax.numpy as jnp
from jax import lax
from jax.experimental import pallas as pl
from jax.experimental.pallas import tpu as pltpu
from jax.sharding import PartitionSpec as P

H = 64
KVH = 4
DH = 128
TILE = 128
STEPS = 64
LOW = -1e30
MESH = pl.DeviceIdType.MESH


def repeat(count, body):
    if count <= 32:
        for index in range(count):
            body(index)
    else:
        lax.fori_loop(0, count, lambda index, nothing: (body(index), nothing)[1], 0)


def attend(q, kv_ref, bias_ref, head, heads, peers, scale):
    depth = kv_ref.shape[1]
    rows = q.shape[0]
    copies = rows // bias_ref.shape[0]
    span = min(peers, max(1, 512 // depth))

    def piece(first):
        keys = kv_ref[pl.ds(first, span), :, head * DH : (head + 1) * DH]
        values = kv_ref[pl.ds(first, span), :, (heads + head) * DH : (heads + head + 1) * DH]
        keys = keys.reshape(span * depth, DH)
        values = values.reshape(span * depth, DH)
        values = jnp.concatenate([values, jnp.ones_like(values)], axis=1)
        scores = lax.dot_general(q, keys, (((1,), (1,)), ((), ())), preferred_element_type=jnp.float32)
        return scores * scale, values

    if span == peers:
        scores, values = piece(0)
        bias = bias_ref[...]
        scores = scores + jnp.concatenate([bias] * copies, axis=0)
        top = jnp.max(scores, axis=1, keepdims=True)
        weights = jnp.exp2(scores - top).astype(jnp.bfloat16)
        both = jnp.dot(weights, values, preferred_element_type=jnp.float32)
    else:
        width = span * depth

        def step(index, carry):
            top, both = carry
            scores, values = piece(index * span)
            bias = bias_ref[:, pl.ds(pl.multiple_of(index * width, width), width)]
            scores = scores + jnp.concatenate([bias] * copies, axis=0)
            newest = jnp.maximum(top, jnp.max(scores, axis=1, keepdims=True))
            weights = jnp.where(scores > 0.5 * LOW, jnp.exp2(scores - newest), 0.0).astype(jnp.bfloat16)
            both = both * jnp.exp2(top - newest) + jnp.dot(weights, values, preferred_element_type=jnp.float32)
            return newest, both

        top = jnp.full((rows, 1), LOW, jnp.float32)
        top, both = lax.fori_loop(0, peers // span, step, (top, jnp.zeros((rows, 2 * DH), jnp.float32)))
    return both[:, :DH] / both[:, DH:]


def kernel(
    row_count, columns, q_hbm, k_hbm, v_hbm, tile_hbm, qstep_hbm, kstep_hbm, out_ref,
    q_ref, send_ref, kv_ref, bias_ref, tile_ref, qstep_ref, kstep_ref, load_sem, send_sem, recv_sem,
):
    peers = row_count * columns
    heads = KVH // columns
    half = heads * DH
    groups = H // KVH
    depth = k_hbm.shape[0]
    keys = peers * depth
    query_count = q_ref.shape[0]
    row = lax.axis_index("row")
    col = lax.axis_index("col")
    me = row * columns + col

    def load(source, target, index):
        copy = pltpu.make_async_copy(source, target, load_sem.at[index])
        copy.start()
        return copy

    own_loads = [load(kstep_hbm, kstep_ref, 0)]
    for other in range(columns):
        span = slice(other * half, (other + 1) * half)
        own_loads.append(load(k_hbm.at[:, span], send_ref.at[other, :, pl.ds(0, half)], 4 + 2 * other))
        own_loads.append(load(v_hbm.at[:, span], send_ref.at[other, :, pl.ds(half, half)], 5 + 2 * other))

    def place(distance):
        peer = lax.rem(me + distance + 1, peers)
        return peer, peer // columns, lax.rem(peer, columns)

    barrier = pltpu.get_barrier_semaphore()

    def greet(distance):
        peer, peer_row, peer_col = place(distance)
        pl.semaphore_signal(barrier, inc=1, device_id={"row": peer_row, "col": peer_col}, device_id_type=MESH)

    repeat(peers - 1, greet)

    other_loads = [load(q_hbm, q_ref, 1), load(qstep_hbm, qstep_ref, 2), load(tile_hbm, tile_ref, 3)]
    own_loads[0].wait()
    steps = kstep_ref[...].astype(jnp.float32)
    eye = lax.broadcasted_iota(jnp.int32, (depth, depth), 0) == lax.broadcasted_iota(jnp.int32, (depth, depth), 1)
    column = jnp.sum(jnp.where(eye, jnp.broadcast_to(steps, (depth, depth)), 0.0), axis=1, keepdims=True)
    marks = jnp.broadcast_to(column, (depth, DH)).astype(jnp.bfloat16)
    for other in range(columns):
        send_ref[other, :, 2 * half :] = marks
    for copy in own_loads[1:]:
        copy.wait()
    pl.semaphore_wait(barrier, peers - 1)

    def copy_to(peer, peer_row, peer_col):
        return pltpu.make_async_remote_copy(
            src_ref=send_ref.at[peer_col],
            dst_ref=kv_ref.at[me],
            send_sem=send_sem.at[peer],
            recv_sem=recv_sem.at[me],
            device_id={"row": peer_row, "col": peer_col},
            device_id_type=MESH,
        )

    repeat(peers - 1, lambda distance: copy_to(*place(distance)).start())

    def receive(distance):
        peer, peer_row, peer_col = place(distance)
        pltpu.make_async_remote_copy(
            src_ref=send_ref.at[0],
            dst_ref=kv_ref.at[peer],
            send_sem=send_sem.at[peer],
            recv_sem=recv_sem.at[peer],
            device_id={"row": peer_row, "col": peer_col},
            device_id_type=MESH,
        ).wait_recv()

    kv_ref[me] = send_ref[col]
    for copy in other_loads:
        copy.wait()
    repeat(peers - 1, receive)

    marks = kv_ref[:, :, 2 * half :].reshape(keys, DH).astype(jnp.float32)
    lane = lax.broadcasted_iota(jnp.int32, (keys, DH), 1).astype(jnp.float32)
    late = jnp.where(marks > lane, LOW, 0.0).astype(jnp.bfloat16)
    picked = lax.broadcasted_iota(jnp.int32, (DH, query_count), 0) == qstep_ref[...]
    picked = jnp.where(picked, 1.0, 0.0).astype(jnp.bfloat16)
    bias = lax.dot_general(picked, late, (((0,), (1,)), ((), ())), preferred_element_type=jnp.float32)
    first_row = row * query_count
    key_tiles = tile_ref.shape[0]
    block = min(TILE, query_count)
    for part in range(query_count // block):
        tile = (first_row + part * block) // TILE
        for key_tile in range(key_tiles):
            closed = jnp.where(tile_ref[key_tile, tile] == 1, 0.0, LOW)
            span = slice(key_tile * TILE, (key_tile + 1) * TILE)
            bias_ref[part * block : (part + 1) * block, span] = (
                bias[part * block : (part + 1) * block, span] + closed
            )

    scale = math.log2(math.e) / math.sqrt(DH)
    together = max(1, min(groups, 256 // query_count))
    for head in range(heads):
        for start in range(0, groups, together):
            base = (head * groups + start) * DH
            q = jnp.concatenate(
                [q_ref[:, base + g * DH : base + (g + 1) * DH] for g in range(together)], axis=0
            )
            result = attend(q, kv_ref, bias_ref, head, heads, peers, scale).astype(jnp.bfloat16)
            for g in range(together):
                out_ref[:, base + g * DH : base + (g + 1) * DH] = result[
                    g * query_count : (g + 1) * query_count
                ]

    repeat(peers - 1, lambda distance: copy_to(*place(distance)).wait_send())


def solution(mesh):
    row_count, columns = mesh.shape["row"], mesh.shape["col"]
    peers = row_count * columns

    def per_device(queries, key_cache, value_cache, tile_active, query_step, key_step):
        depth = key_cache.shape[0]
        width = 2 * (KVH // columns) * DH + DH
        vmem = pl.BlockSpec(memory_space=pltpu.VMEM)
        return pl.pallas_call(
            functools.partial(kernel, row_count, columns),
            out_shape=jax.ShapeDtypeStruct(queries.shape, jnp.bfloat16),
            in_specs=[pl.BlockSpec(memory_space=pltpu.HBM)] * 6,
            out_specs=vmem,
            scratch_shapes=[
                pltpu.VMEM(queries.shape, jnp.bfloat16),
                pltpu.VMEM((columns, depth, width), jnp.bfloat16),
                pltpu.VMEM((peers, depth, width), jnp.bfloat16),
                pltpu.VMEM((queries.shape[0], peers * depth), jnp.float32),
                pltpu.SMEM(tile_active.shape[::-1], jnp.int32),
                pltpu.VMEM((1, query_step.shape[0]), jnp.int32),
                pltpu.VMEM((1, depth), jnp.int32),
                pltpu.SemaphoreType.DMA((4 + 2 * columns,)),
                pltpu.SemaphoreType.DMA((peers,)),
                pltpu.SemaphoreType.DMA((peers,)),
            ],
            compiler_params=pltpu.CompilerParams(
                collective_id=0, has_side_effects=True, vmem_limit_bytes=64 * 1024 * 1024
            ),
        )(queries, key_cache, value_cache, tile_active.T, query_step[None, :], key_step[None, :])

    in_specs = (
        P(("grp", "row"), "col"),
        P(("grp", "row", "col"), None),
        P(("grp", "row", "col"), None),
        P("grp", None),
        P(("grp", "row")),
        P(("grp", "row", "col")),
    )
    return jax.shard_map(
        per_device, mesh=mesh, in_specs=in_specs, out_specs=P(("grp", "row"), "col"), check_vma=False
    )
```
